32 devices in a mesh: dp: 8 (over z, core), tensor: 4 (over y, x).
Axes of the slice: x: 2, y: 2, z: 4, core: 2. Of those that a mesh axis runs over, the one named last changes fastest.
Arguments:
- patches: bfloat16 [8192, 3200], P('dp', 'tensor'), may hold values from -40 to 40
- encoder_row: int32 [8192], P('dp'), may hold values from 0 to 8191, as said below
- norm_gain: bfloat16 [3200], P('tensor'), may hold values from 0.5 to 1.5
- joint_weight: bfloat16 [3200, 6144], P(None, 'tensor'), may hold values from -8 to 8
- out_weight: bfloat16 [2048, 3200], P(None, 'tensor'), may hold values from -0.1875 to 0.1875
- layer_scale: bfloat16 [3200], P('tensor'), may hold values from 1 to 8
- pos_embed: bfloat16 [1024, 3200], P(None, 'tensor'), may hold values from -3 to 3
Outputs:
- encoded: bfloat16 [8192, 3200], P('dp', 'tensor')
The draws below stay inside these ranges and needn't reach their ends.
Inputs may be any that keep to these rules, and one draw needn't show every extreme that they name: `encoder_row`: A bijection from the rows of patches onto the encoder rows; device d's encoder batch is rows d * 1024 to (d + 1) * 1024 - 1. The rows of each aligned block of 1024 rows of the packed stream (one tile) map onto one aligned block of 1024 encoder rows, and a row's encoder row is congruent to its shard's index modulo 8.
All inputs are finite; a program needn't handle non-finite values.
Results may differ from the reference program's by a relative error of at most 0.0058.
Values may be sent and summed in bfloat16 or wider, within the bound.
A program may use at most 128 MiB of HBM per device.

```python
import math
import jax
import jax.numpy as jnp
from jax import lax

D = 3200
HEADS = 16
HD = 128
UNIT = 1024
E_DEV = 1024
TOKENS = 8192
N_DP = 8


def draw_encoder_row(key, part):
    key = jax.random.fold_in(key, 1)
    block_len = UNIT
    block_count = TOKENS // block_len
    slot_count = UNIT // N_DP
    shuffle = jax.random.permutation(jax.random.fold_in(key, 11), block_count)
    rotation = jax.random.randint(jax.random.fold_in(key, 13), (block_count,), 0, slot_count)
    index = jnp.arange(TOKENS, dtype=jnp.int32)
    shard = index // E_DEV
    within = index % E_DEV
    stream = within * N_DP + shard
    stream_block = stream // block_len
    offset = stream % block_len
    moved = offset % N_DP + N_DP * ((offset // N_DP + rotation[stream_block]) % slot_count)
    return (shuffle[stream_block] * block_len + moved).astype(jnp.int32)


def draw_patches(key, part):
    key = jax.random.fold_in(key, 3)
    first = jax.random.fold_in(key, 0)
    columns = jnp.arange(D, dtype=jnp.float32) / D
    base = jnp.clip(jax.random.normal(first, (TOKENS, D), jnp.float32), -5.0, 5.0)
    values = base * jnp.exp(0.5 * columns * math.log(3.0))[None, :]
    return values.astype(jnp.bfloat16)


def draw_joint_weight(key, part):
    key = jax.random.fold_in(key, 5)
    first, second, third = jax.random.split(key, 3)
    shape = (D, HEADS, 1, HD)
    drawn = D ** (-0.5)
    queries = jnp.clip(jax.random.normal(first, shape, jnp.float32), -5.0, 5.0) * drawn
    key_vecs = jnp.clip(jax.random.normal(second, shape, jnp.float32), -5.0, 5.0) * drawn
    values = jnp.clip(jax.random.normal(third, shape, jnp.float32), -5.0, 5.0) * drawn
    joined = jnp.concatenate([queries, key_vecs, values], axis=2)
    return joined.reshape(D, HEADS * 3 * HD).astype(jnp.bfloat16)


def raised(values, own_key, source, target, blocks, factor):
    def block_of(axis_at):
        return (jnp.arange(values.shape[axis_at]) // (values.shape[axis_at] // blocks)).reshape((-1,) + (1,) * (values.ndim - 1 - axis_at))

    one_side = jax.random.permutation(own_key, blocks)[block_of(target)]
    far = (block_of(target) + blocks // 2) % blocks
    return jnp.where((block_of(source) == one_side) | (block_of(source) == far), factor * values, values)


def shard_levels(key, extent, shards, least, high):
    loudness = 1.0
    for axis_at, parts in shards:
        steps = jax.random.uniform(jax.random.fold_in(jax.random.fold_in(key, 6), axis_at), (parts,), jnp.float32, least / len(shards), high / len(shards))
        loudness = loudness * jnp.repeat(jnp.exp(steps), extent[axis_at] // parts).reshape((-1,) + (1,) * (len(extent) - 1 - axis_at))
    return loudness


def bell_draw(key, dims, deviation, limit, shards=(), kind=jnp.bfloat16):
    loudness = shard_levels(key, dims, shards, -0.22, 0.18) if shards else 1.0
    drawn = jax.random.normal(key, dims, jnp.float32) * deviation * loudness
    return jnp.minimum(jnp.maximum(drawn, -limit), limit).astype(kind)


def heavy_noise(own_key, dims, scale, reach, cuts, heavy, held_as=jnp.bfloat16):
    result = scale * jax.random.normal(own_key, dims, jnp.float32)
    if cuts:
        result = result * shard_levels(own_key, dims, cuts, -0.22, 0.18)
    return jnp.clip(raised(result, jax.random.fold_in(own_key, 3), *heavy), -reach, reach).astype(held_as)


def setup_inputs(seed: int = 0) -> dict:
    key_list = jax.random.split(jax.random.key(seed), 8)
    patches = draw_patches(jax.random.fold_in(key_list[7], 71), 0)
    encoder_row = draw_encoder_row(jax.random.fold_in(key_list[7], 71), 0)
    norm_gain = jnp.clip(1.0 + 0.1 * jax.random.normal(key_list[2], (D,), jnp.float32), 0.5, 1.5).astype(jnp.bfloat16)
    joint_weight = draw_joint_weight(jax.random.fold_in(key_list[7], 71), 0)
    out_weight = heavy_noise(key_list[4], (HEADS * HD, D), (HEADS * HD) ** -0.5, 0.1875, ((1, 4),), (0, 1, 4, 2.0))
    layer_scale = jnp.clip(jnp.exp(math.log(8.0) - 2.0794415 * jax.random.uniform(key_list[5], (D,), jnp.float32) ** shard_levels(key_list[5], (D,), ((0, 4),), -0.2, 0.2)), 1.0, 8.0).astype(jnp.bfloat16)
    pos_embed = bell_draw(key_list[6], (UNIT, D), 0.5, 3.0, ((1, 4),))
    return dict(patches=patches, encoder_row=encoder_row, norm_gain=norm_gain, joint_weight=joint_weight, out_weight=out_weight, layer_scale=layer_scale, pos_embed=pos_embed)


epsilon = 1e-06

def encode_block(block_rows, norm_gain, joint_weight, out_weight, layer_scale):
    block_len = block_rows.shape[0]
    full_feats = block_rows.astype(jnp.float32)
    square_mean = lax.optimization_barrier(jnp.mean(full_feats * full_feats, axis=-1, keepdims=True))
    scaled = (full_feats * norm_gain.astype(jnp.float32)).astype(jnp.bfloat16)
    joint_proj = jnp.dot(scaled, joint_weight, preferred_element_type=jnp.float32) * lax.rsqrt(square_mean + epsilon)
    joint_proj = joint_proj.astype(jnp.bfloat16).reshape(block_len, HEADS, 3, HD).astype(jnp.float32)
    queries = joint_proj[:, :, 0]
    key_vecs = joint_proj[:, :, 1]
    values = joint_proj[:, :, 2]
    scores = jnp.einsum('qhd,khd->hqk', queries, key_vecs) * HD ** (-0.5)
    row_peak = lax.optimization_barrier(jnp.max(scores, axis=-1, keepdims=True))
    exponent = jnp.exp(scores - row_peak)
    weights = (exponent / lax.optimization_barrier(jnp.sum(exponent, axis=-1, keepdims=True))).astype(jnp.bfloat16).astype(jnp.float32)
    attended = jnp.einsum('hqk,khd->qhd', weights, values).astype(jnp.bfloat16).reshape(block_len, HEADS * HD)
    merged = jnp.dot(attended, out_weight, preferred_element_type=jnp.float32)
    return (full_feats + layer_scale.astype(jnp.float32) * merged).astype(jnp.bfloat16)

def reference(patches, encoder_row, norm_gain, joint_weight, out_weight, layer_scale, pos_embed):
    block_len = UNIT
    block_count = TOKENS // block_len
    routed = jnp.zeros_like(patches).at[encoder_row].set(patches)
    blocks = routed.reshape(block_count, block_len, D).astype(jnp.float32)
    blocks = (blocks + pos_embed.astype(jnp.float32)[None]).astype(jnp.bfloat16)

    def inner(block_rows):
        return encode_block(block_rows, norm_gain, joint_weight, out_weight, layer_scale)
    encoded_rows = lax.map(inner, blocks).reshape(TOKENS, D)
    return encoded_rows[encoder_row]
```

```python
import functools

import jax
import jax.numpy as jnp
from jax import lax
from jax.sharding import PartitionSpec as P

HD = 128
UNIT = 1024
EPS = 1e-06


def plain(patches, encoder_row, norm_gain, joint_weight, out_weight, layer_scale, pos_embed):
    peers = lax.axis_size("dp")
    rows, cols = patches.shape
    heads = joint_weight.shape[1] // (3 * HD)
    tiles = rows // UNIT
    per = UNIT // peers

    def swap(x):
        wide = x.shape[-1]
        x = x.reshape(peers, tiles * per, wide)
        return lax.all_to_all(x, "dp", split_axis=0, concat_axis=0, tiled=True)

    pos = pos_embed[encoder_row % UNIT].astype(jnp.float32)
    mine = (patches.astype(jnp.float32) + pos).astype(jnp.bfloat16)
    tile_rows = swap(mine).reshape(peers, tiles, per, cols)
    tile_rows = jnp.swapaxes(tile_rows, 0, 1).reshape(rows, cols)
    full = lax.all_gather(tile_rows, "tensor", axis=1, tiled=True).astype(jnp.float32)
    gain = lax.all_gather(norm_gain, "tensor", axis=0, tiled=True).astype(jnp.float32)
    square_mean = jnp.mean(full * full, axis=-1, keepdims=True)
    scaled = (full * gain).astype(jnp.bfloat16)
    proj = jnp.dot(scaled, joint_weight, preferred_element_type=jnp.float32)
    proj = (proj * lax.rsqrt(square_mean + EPS)).astype(jnp.bfloat16)
    proj = proj.reshape(tiles, UNIT, heads, 3, HD)
    q, k, v = proj[:, :, :, 0], proj[:, :, :, 1], proj[:, :, :, 2]
    scores = jnp.einsum("bqhd,bkhd->bhqk", q, k, preferred_element_type=jnp.float32) * HD ** (-0.5)
    e = jnp.exp(scores - jnp.max(scores, axis=-1, keepdims=True))
    weights = (e / jnp.sum(e, axis=-1, keepdims=True)).astype(jnp.bfloat16)
    att = jnp.einsum("bhqk,bkhd->bqhd", weights, v, preferred_element_type=jnp.float32)
    att = att.astype(jnp.bfloat16).reshape(tiles, peers, per, heads * HD)
    back = swap(jnp.swapaxes(att, 0, 1).reshape(rows, heads * HD)).reshape(rows, heads * HD)
    back = lax.all_gather(back, "tensor", axis=1, tiled=True)
    merged = jnp.dot(back, out_weight, preferred_element_type=jnp.float32)
    return (mine.astype(jnp.float32) + layer_scale.astype(jnp.float32) * merged).astype(jnp.bfloat16)


def solution(mesh):
    body = plain
    placed = (
        P("dp", "tensor"),
        P("dp"),
        P("tensor"),
        P(None, "tensor"),
        P(None, "tensor"),
        P("tensor"),
        P(None, "tensor"),
    )
    return jax.shard_map(
        body, mesh=mesh, in_specs=placed, out_specs=P("dp", "tensor"), check_vma=False
    )
```

```python
import jax
import jax.numpy as jnp
from jax import lax
from jax.experimental import pallas as pl
from jax.experimental.pallas import tpu as pltpu
from jax.sharding import PartitionSpec as P

HD = 128
UNIT = 1024
EPS = 1e-06
MESH = pl.DeviceIdType.MESH


def plain(patches, encoder_row, norm_gain, joint_weight, out_weight, layer_scale, pos_embed):
    peers = lax.axis_size("dp")
    rows, cols = patches.shape
    heads = joint_weight.shape[1] // (3 * HD)
    tiles = rows // UNIT
    per = UNIT // peers

    def swap(x):
        wide = x.shape[-1]
        x = x.reshape(peers, tiles * per, wide)
        return lax.all_to_all(x, "dp", split_axis=0, concat_axis=0, tiled=True)

    pos = pos_embed[encoder_row % UNIT].astype(jnp.float32)
    mine = (patches.astype(jnp.float32) + pos).astype(jnp.bfloat16)
    tile_rows = swap(mine).reshape(peers, tiles, per, cols)
    tile_rows = jnp.swapaxes(tile_rows, 0, 1).reshape(rows, cols)
    full = lax.all_gather(tile_rows, "tensor", axis=1, tiled=True).astype(jnp.float32)
    gain = lax.all_gather(norm_gain, "tensor", axis=0, tiled=True).astype(jnp.float32)
    square_mean = jnp.mean(full * full, axis=-1, keepdims=True)
    scaled = (full * gain).astype(jnp.bfloat16)
    proj = jnp.dot(scaled, joint_weight, preferred_element_type=jnp.float32)
    proj = (proj * lax.rsqrt(square_mean + EPS)).astype(jnp.bfloat16)
    proj = proj.reshape(tiles, UNIT, heads, 3, HD)
    q, k, v = proj[:, :, :, 0], proj[:, :, :, 1], proj[:, :, :, 2]
    scores = jnp.einsum("bqhd,bkhd->bhqk", q, k, preferred_element_type=jnp.float32) * HD ** (-0.5)
    e = jnp.exp(scores - jnp.max(scores, axis=-1, keepdims=True))
    weights = (e / jnp.sum(e, axis=-1, keepdims=True)).astype(jnp.bfloat16)
    att = jnp.einsum("bhqk,bkhd->bqhd", weights, v, preferred_element_type=jnp.float32)
    att = att.astype(jnp.bfloat16).reshape(tiles, peers, per, heads * HD)
    back = swap(jnp.swapaxes(att, 0, 1).reshape(rows, heads * HD)).reshape(rows, heads * HD)
    back = lax.all_gather(back, "tensor", axis=1, tiled=True)
    merged = jnp.dot(back, out_weight, preferred_element_type=jnp.float32)
    return (mine.astype(jnp.float32) + layer_scale.astype(jnp.float32) * merged).astype(jnp.bfloat16)


LINKS = 4


def fused(patches, rows, gain, w_hbm, ow_hbm, scale, pos, out,
          own, mine, feats, w, ow, w_tail, qkv, att, ret, tmp,
          load, send, recv):
    n, per, wide = own.shape
    cols = patches.shape[1]
    full = cols // 128 * 128
    rest = cols - full
    quarters = feats.shape[0]
    depth = w.shape[0]
    heads = w.shape[1] // (3 * HD)
    hw = heads * HD

    s = lax.axis_index("dp")
    t = lax.axis_index("tensor")
    z, core = lax.div(s, 2), lax.rem(s, 2)
    z_hi, z_lo = lax.div(z, 2), lax.rem(z, 2)
    y, x = lax.div(t, 2), lax.rem(t, 2)
    t_x = 2 * y + (1 - x)
    t_y = 2 * (1 - y) + x
    t_d = 2 * (1 - y) + (1 - x)

    def chip(j):
        return 2 * (z_hi if j < 2 else 1 - z_hi) + (z_lo if j % 2 == 0 else 1 - z_lo)

    def peer(k):
        return 2 * chip(k // 2) + (core if k % 2 == 0 else 1 - core)

    def remote(src, dst, kind, i, o, device):
        return pltpu.make_async_remote_copy(
            src_ref=src, dst_ref=dst, send_sem=send.at[kind, i], recv_sem=recv.at[kind, o],
            device_id=device, device_id_type=MESH)

    barrier = pltpu.get_barrier_semaphore()
    for k in range(1, n):
        pl.semaphore_signal(barrier, inc=1, device_id=(peer(k), t), device_id_type=MESH)
    for other in (t_x, t_y):
        pl.semaphore_signal(barrier, inc=1, device_id=(s, other), device_id_type=MESH)

    load_w = pltpu.make_async_copy(w_hbm, w, load.at[0])
    load_ow = pltpu.make_async_copy(ow_hbm, ow, load.at[1])
    load_w.start()
    load_ow.start()

    def prepare(d):
        at = pl.ds(pl.multiple_of(d * per, per), per)
        idx = lax.rem(rows[pl.ds(d, 1), :], UNIT)
        hot = lax.broadcasted_iota(jnp.int32, (UNIT, per), 0) == idx
        hot = jnp.where(hot, 1.0, 0.0).astype(jnp.bfloat16)
        slot = lax.dot_general(hot, pos[...], (((0,), (0,)), ((), ())), preferred_element_type=jnp.float32)
        row = (patches[at, :].astype(jnp.float32) + slot).astype(jnp.bfloat16)
        mine[at, :] = row
        row = row.astype(jnp.float32)
        square = jnp.sum(row * row, axis=-1, keepdims=True)
        scaled = row * gain[...].astype(jnp.float32)
        tmp[:, full:] = jnp.zeros((per, wide - full), jnp.float32)
        tmp[:, :cols] = scaled
        own[d, :, :full] = tmp[:, :full].astype(jnp.bfloat16)
        first = square.astype(jnp.bfloat16).astype(jnp.float32)
        second = (square - first).astype(jnp.bfloat16).astype(jnp.float32)
        third = square - first - second
        lane = lax.broadcasted_iota(jnp.int32, (per, wide - full), 1)
        last = jnp.where(lane == rest, first, jnp.where(lane == rest + 1, second, jnp.where(lane == rest + 2, third, tmp[:, full:])))
        own[d, :, full:] = last.astype(jnp.bfloat16)

    def scatter(buf, src, base, k):
        d = peer(k)
        remote(src.at[d], buf.at[t, s], base, d, s, (d, t)).start()

    def direct(buf, base, k):
        i = peer(k)
        if k > 0:
            remote(buf.at[t, i], buf.at[t, i], base, i, i, (s, t)).wait_recv()
        remote(buf.at[t, i], buf.at[t, i], base + 1, i, i, (s, t_x)).start()
        remote(buf.at[t, i], buf.at[t, i], base + 2, i, i, (s, t_y)).start()

    def relay(buf, base, k):
        i = peer(k)
        remote(buf.at[t, i], buf.at[t_x, i], base + 1, i, i, (s, t_x)).wait_recv()
        remote(buf.at[t, i], buf.at[t_y, i], base + 2, i, i, (s, t_y)).wait_recv()
        if k % 2 == 0:
            remote(buf.at[t_x, i], buf.at[t_x, i], base + 3, i, i, (s, t_y)).start()
        else:
            remote(buf.at[t_y, i], buf.at[t_y, i], base + 3, i, i, (s, t_x)).start()

    def settle(buf, base, k):
        i = peer(k)
        remote(buf.at[t_d, i], buf.at[t_d, i], base + 3, i, i, (s, t_x)).wait_recv()

    def project(j):
        settle(feats, 0, 2 * j)
        settle(feats, 0, 2 * j + 1)
        zj = chip(j)
        two = pl.ds(2 * zj, 2)
        at = pl.ds(pl.multiple_of(zj * 2 * per, 2 * per), 2 * per)
        lane = lax.broadcasted_iota(jnp.int32, (2 * per, 128), 1)
        tail = jnp.zeros((2 * per, 128), jnp.float32)
        square = jnp.zeros((2 * per, 128), jnp.float32)
        for q in range(quarters):
            last = feats[q, two, :, full:].reshape(2 * per, 128).astype(jnp.float32)
            square += jnp.where((lane >= rest) & (lane < rest + 3), last, 0.0)
            moved = last if q == 0 else pltpu.roll(last, rest * q, 1)
            tail = jnp.where((lane >= rest * q) & (lane < rest * (q + 1)), moved, tail)
        tail = tail.astype(jnp.bfloat16)
        norm = lax.rsqrt(jnp.sum(square, axis=-1, keepdims=True) * (1.0 / depth) + EPS)

        def head(h, carry):
            span = pl.ds(pl.multiple_of(h * 3 * HD, 128), 3 * HD)
            acc = jnp.dot(tail, w_tail[:, span], preferred_element_type=jnp.float32)
            for q in range(quarters):
                part = feats[q, two, :, :full].reshape(2 * per, full)
                acc += jnp.dot(part, w[q * cols:q * cols + full, span], preferred_element_type=jnp.float32)
            qkv[at, span] = (acc * norm).astype(jnp.bfloat16)
            return carry

        lax.fori_loop(0, heads, head, 0)

    def attend(j):
        zj = chip(j)
        at = pl.ds(pl.multiple_of(zj * 2 * per, 2 * per), 2 * per)

        def head(h, carry):
            q = qkv[at, pl.ds(pl.multiple_of(h * 3 * HD, 128), HD)]
            k = qkv[:, pl.ds(pl.multiple_of(h * 3 * HD + HD, 128), HD)]
            v = qkv[:, pl.ds(pl.multiple_of(h * 3 * HD + 2 * HD, 128), HD)]
            score = lax.dot_general(q, k, (((1,), (1,)), ((), ())), preferred_element_type=jnp.float32)
            peak = jnp.max(score, axis=-1, keepdims=True)
            e = jnp.exp2((score - peak) * (HD ** (-0.5) * 1.4426950408889634))
            total = jnp.sum(e, axis=-1, keepdims=True)
            o = jnp.dot(e.astype(jnp.bfloat16), v, preferred_element_type=jnp.float32) / total
            att[pl.ds(2 * zj, 2), :, pl.ds(pl.multiple_of(h * HD, 128), HD)] = o.astype(jnp.bfloat16).reshape(2, per, HD)
            return carry

        lax.fori_loop(0, heads, head, 0)

    def finish(j):
        settle(ret, LINKS, 2 * j)
        settle(ret, LINKS, 2 * j + 1)
        zj = chip(j)
        at = pl.ds(pl.multiple_of(zj * 2 * per, 2 * per), 2 * per)
        acc = jnp.zeros((2 * per, cols), jnp.float32)
        for q in range(quarters):
            part = ret[q, pl.ds(2 * zj, 2)].reshape(2 * per, hw)
            acc += jnp.dot(part, ow[q * hw:(q + 1) * hw, :], preferred_element_type=jnp.float32)
        out[at, :] = (mine[at, :].astype(jnp.float32) + scale[...].astype(jnp.float32) * acc).astype(jnp.bfloat16)

    prepare(s)
    feats[t, s] = own[s]
    pl.semaphore_wait(barrier, n + 1)
    direct(feats, 0, 0)
    for k in range(1, n):
        prepare(peer(k))
        scatter(feats, own, 0, k)
    load_w.wait()
    for q in range(quarters):
        w_tail[q * rest:(q + 1) * rest, :] = w[q * cols + full:(q + 1) * cols, :]
    for k in range(1, n):
        direct(feats, 0, k)
        relay(feats, 0, k - 1)
        if k >= 3 and k % 2 == 1:
            project((k - 3) // 2)
    relay(feats, 0, n - 1)
    project(n // 2 - 1)

    pairs = n // 2
    load_ow.wait()
    for j in range(pairs + 2):
        if j < pairs:
            attend(j)
            for k in (2 * j, 2 * j + 1):
                if k == 0:
                    ret[t, s] = att[s]
                    direct(ret, LINKS, 0)
                else:
                    scatter(ret, att, LINKS, k)
        if 1 <= j <= pairs:
            for k in (2 * j - 2, 2 * j - 1):
                if k > 0:
                    direct(ret, LINKS, k)
            for k in (2 * j - 2, 2 * j - 1):
                relay(ret, LINKS, k)
        if j >= 2:
            finish(j - 2)

    for k in range(n):
        i = peer(k)
        for base, buf, src in ((0, feats, own), (LINKS, ret, att)):
            for kind in range(LINKS):
                if kind > 0 or k > 0:
                    whole = src.at[i] if kind == 0 else buf.at[t, i]
                    remote(whole, whole, base + kind, i, i, (s, t_x)).wait_send()


def one_kernel(patches, encoder_row, norm_gain, joint_weight, out_weight, layer_scale, pos_embed):
    n, quarters = lax.axis_size("dp"), lax.axis_size("tensor")
    rows, cols = patches.shape
    per = rows // n
    wide = -(-cols // 128) * 128
    hw = out_weight.shape[0] // quarters
    vmem = pl.BlockSpec(memory_space=pltpu.VMEM)
    hbm = pl.BlockSpec(memory_space=pl.ANY)
    bf16 = jnp.bfloat16
    return pl.pallas_call(
        fused,
        out_shape=jax.ShapeDtypeStruct((rows, cols), bf16),
        in_specs=[vmem, vmem, vmem, hbm, hbm, vmem, vmem],
        out_specs=vmem,
        scratch_shapes=[
            pltpu.VMEM((n, per, wide), bf16),
            pltpu.VMEM((rows, cols), bf16),
            pltpu.VMEM((quarters, n, per, wide), bf16),
            pltpu.VMEM(joint_weight.shape, bf16),
            pltpu.VMEM(out_weight.shape, bf16),
            pltpu.VMEM((128, joint_weight.shape[1]), bf16),
            pltpu.VMEM((rows, joint_weight.shape[1]), bf16),
            pltpu.VMEM((n, per, hw), bf16),
            pltpu.VMEM((quarters, n, per, hw), bf16),
            pltpu.VMEM((per, wide), jnp.float32),
            pltpu.SemaphoreType.DMA((2,)),
            pltpu.SemaphoreType.DMA((2 * LINKS, n)),
            pltpu.SemaphoreType.DMA((2 * LINKS, n)),
        ],
        compiler_params=pltpu.CompilerParams(
            collective_id=0, has_side_effects=True, vmem_limit_bytes=60 * 1024 * 1024),
    )(patches, encoder_row.reshape(n, per), norm_gain.reshape(1, cols), joint_weight, out_weight,
      layer_scale.reshape(1, cols), pos_embed)


def solution(mesh):
    fits = dict(mesh.shape) == dict(dp=8, tensor=4)
    body = one_kernel if fits else plain
    placed = (
        P("dp", "tensor"),
        P("dp"),
        P("tensor"),
        P(None, "tensor"),
        P(None, "tensor"),
        P("tensor"),
        P(None, "tensor"),
    )
    return jax.shard_map(
        body, mesh=mesh, in_specs=placed, out_specs=P("dp", "tensor"), check_vma=False
    )
```

```python
import jax
import jax.numpy as jnp
from jax import lax
from jax.experimental import pallas as pl
from jax.experimental.pallas import tpu as pltpu
from jax.sharding import PartitionSpec as P

HD = 128
UNIT = 1024
EPS = 1e-06
MESH = pl.DeviceIdType.MESH


def plain(patches, encoder_row, norm_gain, joint_weight, out_weight, layer_scale, pos_embed):
    peers = lax.axis_size("dp")
    rows, cols = patches.shape
    heads = joint_weight.shape[1] // (3 * HD)
    tiles = rows // UNIT
    per = UNIT // peers

    def swap(x):
        wide = x.shape[-1]
        x = x.reshape(peers, tiles * per, wide)
        return lax.all_to_all(x, "dp", split_axis=0, concat_axis=0, tiled=True)

    pos = pos_embed[encoder_row % UNIT].astype(jnp.float32)
    mine = (patches.astype(jnp.float32) + pos).astype(jnp.bfloat16)
    tile_rows = swap(mine).reshape(peers, tiles, per, cols)
    tile_rows = jnp.swapaxes(tile_rows, 0, 1).reshape(rows, cols)
    full = lax.all_gather(tile_rows, "tensor", axis=1, tiled=True).astype(jnp.float32)
    gain = lax.all_gather(norm_gain, "tensor", axis=0, tiled=True).astype(jnp.float32)
    square_mean = jnp.mean(full * full, axis=-1, keepdims=True)
    scaled = (full * gain).astype(jnp.bfloat16)
    proj = jnp.dot(scaled, joint_weight, preferred_element_type=jnp.float32)
    proj = (proj * lax.rsqrt(square_mean + EPS)).astype(jnp.bfloat16)
    proj = proj.reshape(tiles, UNIT, heads, 3, HD)
    q, k, v = proj[:, :, :, 0], proj[:, :, :, 1], proj[:, :, :, 2]
    scores = jnp.einsum("bqhd,bkhd->bhqk", q, k, preferred_element_type=jnp.float32) * HD ** (-0.5)
    e = jnp.exp(scores - jnp.max(scores, axis=-1, keepdims=True))
    weights = (e / jnp.sum(e, axis=-1, keepdims=True)).astype(jnp.bfloat16)
    att = jnp.einsum("bhqk,bkhd->bqhd", weights, v, preferred_element_type=jnp.float32)
    att = att.astype(jnp.bfloat16).reshape(tiles, peers, per, heads * HD)
    back = swap(jnp.swapaxes(att, 0, 1).reshape(rows, heads * HD)).reshape(rows, heads * HD)
    back = lax.all_gather(back, "tensor", axis=1, tiled=True)
    merged = jnp.dot(back, out_weight, preferred_element_type=jnp.float32)
    return (mine.astype(jnp.float32) + layer_scale.astype(jnp.float32) * merged).astype(jnp.bfloat16)


LINKS = 4


def fused(patches, rows, sides, w_hbm, ow_hbm, pos, out,
          own, mine, feats, w, ow, w_tail, qkv, att, ret, gain, scale,
          load, send, recv):
    n = own.shape[0]
    cols = patches.shape[0]
    per = patches.shape[1] // n
    full = cols // 128 * 128
    rest = cols - full
    steps = full // 128
    sums = steps * per + rest
    quarters = feats.shape[0]
    depth = w.shape[0]
    heads = w.shape[1] // (3 * HD)
    hw = heads * HD

    s = lax.axis_index("dp")
    t = lax.axis_index("tensor")
    z, core = lax.div(s, 2), lax.rem(s, 2)
    z_hi, z_lo = lax.div(z, 2), lax.rem(z, 2)
    y, x = lax.div(t, 2), lax.rem(t, 2)
    t_x = 2 * y + (1 - x)
    t_y = 2 * (1 - y) + x
    t_d = 2 * (1 - y) + (1 - x)

    def chip(j):
        return 2 * (z_hi if j < 2 else 1 - z_hi) + (z_lo if j % 2 == 0 else 1 - z_lo)

    def peer(k):
        return 2 * chip(k // 2) + (core if k % 2 == 0 else 1 - core)

    def remote(src, dst, kind, i, o, device):
        return pltpu.make_async_remote_copy(
            src_ref=src, dst_ref=dst, send_sem=send.at[kind, i], recv_sem=recv.at[kind, o],
            device_id=device, device_id_type=MESH)

    barrier = pltpu.get_barrier_semaphore()
    for k in range(1, n):
        pl.semaphore_signal(barrier, inc=1, device_id=(peer(k), t), device_id_type=MESH)
    for other in (t_x, t_y):
        pl.semaphore_signal(barrier, inc=1, device_id=(s, other), device_id_type=MESH)

    load_w = pltpu.make_async_copy(w_hbm, w, load.at[0])
    load_ow = pltpu.make_async_copy(ow_hbm, ow, load.at[1])
    load_w.start()
    load_ow.start()

    for which, wide in enumerate((gain, scale)):
        pick = lax.broadcasted_iota(jnp.int32, (16, 128), 0) == which
        pick = jnp.where(pick, 1.0, 0.0).astype(jnp.bfloat16)
        wide[...] = lax.dot_general(sides[...], pick, (((0,), (0,)), ((), ())), preferred_element_type=jnp.float32)

    def prepare(d):
        at = pl.ds(pl.multiple_of(d * per, per), per)
        idx = lax.rem(rows[pl.ds(d, 1), :], UNIT)
        hot = lax.broadcasted_iota(jnp.int32, (UNIT, per), 0) == idx
        hot = jnp.where(hot, 1.0, 0.0).astype(jnp.bfloat16)
        slot = jnp.dot(pos[...], hot, preferred_element_type=jnp.float32)
        row = (patches[:, at].astype(jnp.float32) + slot).astype(jnp.bfloat16)
        mine[:, at] = row
        row = row.astype(jnp.float32)
        square = jnp.sum(row * row, axis=0, keepdims=True)
        scaled = row * gain[...]
        for c in range(steps):
            own[d, c * per:(c + 1) * per, :] = scaled[c * 128:(c + 1) * 128].T.astype(jnp.bfloat16)
        own[d, steps * per:sums, :] = scaled[full:].astype(jnp.bfloat16)
        first = square.astype(jnp.bfloat16).astype(jnp.float32)
        second = (square - first).astype(jnp.bfloat16).astype(jnp.float32)
        third = square - first - second
        at_row = lax.broadcasted_iota(jnp.int32, (16, per), 0)
        last = jnp.where(at_row == 0, first, jnp.where(at_row == 1, second, jnp.where(at_row == 2, third, 0.0)))
        own[d, sums:, :] = last.astype(jnp.bfloat16)

    def scatter(buf, src, base, k):
        d = peer(k)
        remote(src.at[d], buf.at[t, s], base, d, s, (d, t)).start()

    def direct(buf, base, k):
        i = peer(k)
        if k > 0:
            remote(buf.at[t, i], buf.at[t, i], base, i, i, (s, t)).wait_recv()
        remote(buf.at[t, i], buf.at[t, i], base + 1, i, i, (s, t_x)).start()
        remote(buf.at[t, i], buf.at[t, i], base + 2, i, i, (s, t_y)).start()

    def relay(buf, base, k):
        i = peer(k)
        remote(buf.at[t, i], buf.at[t_x, i], base + 1, i, i, (s, t_x)).wait_recv()
        remote(buf.at[t, i], buf.at[t_y, i], base + 2, i, i, (s, t_y)).wait_recv()
        if k % 2 == 0:
            remote(buf.at[t_x, i], buf.at[t_x, i], base + 3, i, i, (s, t_y)).start()
        else:
            remote(buf.at[t_y, i], buf.at[t_y, i], base + 3, i, i, (s, t_x)).start()

    def settle(buf, base, k):
        i = peer(k)
        remote(buf.at[t_d, i], buf.at[t_d, i], base + 3, i, i, (s, t_x)).wait_recv()

    def project(j):
        settle(feats, 0, 2 * j)
        settle(feats, 0, 2 * j + 1)
        zj = chip(j)
        two = pl.ds(2 * zj, 2)
        at = pl.ds(pl.multiple_of(zj * 2 * per, 2 * per), 2 * per)
        def sides_of(low, high):
            return jnp.concatenate(
                [jnp.concatenate([feats[q, 2 * zj + c, low:high, :] for q in range(quarters)], axis=0) for c in range(2)], axis=1)

        tail = sides_of(steps * per, sums)
        square = lax.dot_general(sides_of(sums, sums + 16), jnp.ones((16 * quarters, 128), jnp.bfloat16),
                                 (((0,), (0,)), ((), ())), preferred_element_type=jnp.float32)
        norm = lax.rsqrt(square[:, :1] * (1.0 / depth) + EPS)

        def head(h, carry):
            span = pl.ds(pl.multiple_of(h * 3 * HD, 128), 3 * HD)
            acc = lax.dot_general(tail, w_tail[:, span], (((0,), (0,)), ((), ())), preferred_element_type=jnp.float32)
            for q in range(quarters):
                part = jnp.concatenate([feats[q, two, c * per:(c + 1) * per, :].reshape(2 * per, 128) for c in range(steps)], axis=1)
                acc += jnp.dot(part, w[q * cols:q * cols + full, span], preferred_element_type=jnp.float32)
            qkv[at, span] = (acc * norm).astype(jnp.bfloat16)
            return carry

        lax.fori_loop(0, heads, head, 0)

    def attend(j):
        zj = chip(j)
        at = pl.ds(pl.multiple_of(zj * 2 * per, 2 * per), 2 * per)

        def head(h, carry):
            q = qkv[at, pl.ds(pl.multiple_of(h * 3 * HD, 128), HD)]
            k = qkv[:, pl.ds(pl.multiple_of(h * 3 * HD + HD, 128), HD)]
            v = qkv[:, pl.ds(pl.multiple_of(h * 3 * HD + 2 * HD, 128), HD)]
            score = lax.dot_general(q, k, (((1,), (1,)), ((), ())), preferred_element_type=jnp.float32)
            peak = jnp.max(score, axis=-1, keepdims=True)
            e = jnp.exp2((score - peak) * (HD ** (-0.5) * 1.4426950408889634))
            total = jnp.sum(e, axis=-1, keepdims=True)
            o = jnp.dot(e.astype(jnp.bfloat16), v, preferred_element_type=jnp.float32) / total
            att[pl.ds(2 * zj, 2), :, pl.ds(pl.multiple_of(h * HD, 128), HD)] = o.astype(jnp.bfloat16).reshape(2, per, HD)
            return carry

        lax.fori_loop(0, heads, head, 0)

    def finish(j):
        settle(ret, LINKS, 2 * j)
        settle(ret, LINKS, 2 * j + 1)
        zj = chip(j)
        at = pl.ds(pl.multiple_of(zj * 2 * per, 2 * per), 2 * per)
        acc = jnp.zeros((cols, 2 * per), jnp.float32)
        for q in range(quarters):
            part = ret[q, pl.ds(2 * zj, 2)].reshape(2 * per, hw)
            acc += lax.dot_general(ow[:, q * hw:(q + 1) * hw], part, (((1,), (1,)), ((), ())), preferred_element_type=jnp.float32)
        level = jnp.concatenate([scale[...], scale[...]], axis=1)
        out[:, at] = (mine[:, at].astype(jnp.float32) + level * acc).astype(jnp.bfloat16)

    prepare(s)
    feats[t, s] = own[s]
    pl.semaphore_wait(barrier, n + 1)
    direct(feats, 0, 0)
    for k in range(1, n):
        prepare(peer(k))
        scatter(feats, own, 0, k)
    load_w.wait()
    for q in range(quarters):
        w_tail[q * rest:(q + 1) * rest, :] = w[q * cols + full:(q + 1) * cols, :]
    for k in range(1, n):
        direct(feats, 0, k)
        relay(feats, 0, k - 1)
        if k >= 3 and k % 2 == 1:
            project((k - 3) // 2)
    relay(feats, 0, n - 1)
    project(n // 2 - 1)

    pairs = n // 2
    load_ow.wait()
    for j in range(pairs + 2):
        if j < pairs:
            attend(j)
            for k in (2 * j, 2 * j + 1):
                if k == 0:
                    ret[t, s] = att[s]
                    direct(ret, LINKS, 0)
                else:
                    scatter(ret, att, LINKS, k)
        if 1 <= j <= pairs:
            for k in (2 * j - 2, 2 * j - 1):
                if k > 0:
                    direct(ret, LINKS, k)
            for k in (2 * j - 2, 2 * j - 1):
                relay(ret, LINKS, k)
        if j >= 2:
            finish(j - 2)

    for k in range(n):
        i = peer(k)
        for base, buf, src in ((0, feats, own), (LINKS, ret, att)):
            for kind in range(LINKS):
                if kind > 0 or k > 0:
                    whole = src.at[i] if kind == 0 else buf.at[t, i]
                    remote(whole, whole, base + kind, i, i, (s, t_x)).wait_send()


def one_kernel(patches, encoder_row, norm_gain, joint_weight, out_weight, layer_scale, pos_embed):
    n, quarters = lax.axis_size("dp"), lax.axis_size("tensor")
    rows, cols = patches.shape
    per = rows // n
    packed = cols // 128 * per + cols % 128 + 16
    hw = out_weight.shape[0] // quarters
    vmem = pl.BlockSpec(memory_space=pltpu.VMEM)
    hbm = pl.BlockSpec(memory_space=pl.ANY)
    bf16 = jnp.bfloat16
    sides = jnp.pad(jnp.stack([norm_gain, layer_scale]), ((0, 14), (0, 0)))
    result = pl.pallas_call(
        fused,
        out_shape=jax.ShapeDtypeStruct((cols, rows), bf16),
        in_specs=[vmem, vmem, vmem, hbm, hbm, vmem],
        out_specs=vmem,
        scratch_shapes=[
            pltpu.VMEM((n, packed, 128), bf16),
            pltpu.VMEM((cols, rows), bf16),
            pltpu.VMEM((quarters, n, packed, 128), bf16),
            pltpu.VMEM(joint_weight.shape, bf16),
            pltpu.VMEM((cols, quarters * hw), bf16),
            pltpu.VMEM((128, joint_weight.shape[1]), bf16),
            pltpu.VMEM((rows, joint_weight.shape[1]), bf16),
            pltpu.VMEM((n, per, hw), bf16),
            pltpu.VMEM((quarters, n, per, hw), bf16),
            pltpu.VMEM((cols, 128), jnp.float32),
            pltpu.VMEM((cols, 128), jnp.float32),
            pltpu.SemaphoreType.DMA((2,)),
            pltpu.SemaphoreType.DMA((2 * LINKS, n)),
            pltpu.SemaphoreType.DMA((2 * LINKS, n)),
        ],
        compiler_params=pltpu.CompilerParams(
            collective_id=0, has_side_effects=True, vmem_limit_bytes=60 * 1024 * 1024),
    )(patches.T, encoder_row.reshape(n, per), sides, joint_weight, out_weight.T, pos_embed.T)
    return result.T


def solution(mesh):
    fits = dict(mesh.shape) == dict(dp=8, tensor=4)
    body = one_kernel if fits else plain
    placed = (
        P("dp", "tensor"),
        P("dp"),
        P("tensor"),
        P(None, "tensor"),
        P(None, "tensor"),
        P("tensor"),
        P(None, "tensor"),
    )
    return jax.shard_map(
        body, mesh=mesh, in_specs=placed, out_specs=P("dp", "tensor"), check_vma=False
    )
```

```python
import jax
import jax.numpy as jnp
from jax import lax
from jax.experimental import pallas as pl
from jax.experimental.pallas import tpu as pltpu
from jax.sharding import PartitionSpec as P

HD = 128
UNIT = 1024
EPS = 1e-06
MESH = pl.DeviceIdType.MESH


def plain(patches, encoder_row, norm_gain, joint_weight, out_weight, layer_scale, pos_embed):
    peers = lax.axis_size("dp")
    rows, cols = patches.shape
    heads = joint_weight.shape[1] // (3 * HD)
    tiles = rows // UNIT
    per = UNIT // peers

    def swap(x):
        wide = x.shape[-1]
        x = x.reshape(peers, tiles * per, wide)
        return lax.all_to_all(x, "dp", split_axis=0, concat_axis=0, tiled=True)

    pos = pos_embed[encoder_row % UNIT].astype(jnp.float32)
    mine = (patches.astype(jnp.float32) + pos).astype(jnp.bfloat16)
    tile_rows = swap(mine).reshape(peers, tiles, per, cols)
    tile_rows = jnp.swapaxes(tile_rows, 0, 1).reshape(rows, cols)
    full = lax.all_gather(tile_rows, "tensor", axis=1, tiled=True).astype(jnp.float32)
    gain = lax.all_gather(norm_gain, "tensor", axis=0, tiled=True).astype(jnp.float32)
    square_mean = jnp.mean(full * full, axis=-1, keepdims=True)
    scaled = (full * gain).astype(jnp.bfloat16)
    proj = jnp.dot(scaled, joint_weight, preferred_element_type=jnp.float32)
    proj = (proj * lax.rsqrt(square_mean + EPS)).astype(jnp.bfloat16)
    proj = proj.reshape(tiles, UNIT, heads, 3, HD)
    q, k, v = proj[:, :, :, 0], proj[:, :, :, 1], proj[:, :, :, 2]
    scores = jnp.einsum("bqhd,bkhd->bhqk", q, k, preferred_element_type=jnp.float32) * HD ** (-0.5)
    e = jnp.exp(scores - jnp.max(scores, axis=-1, keepdims=True))
    weights = (e / jnp.sum(e, axis=-1, keepdims=True)).astype(jnp.bfloat16)
    att = jnp.einsum("bhqk,bkhd->bqhd", weights, v, preferred_element_type=jnp.float32)
    att = att.astype(jnp.bfloat16).reshape(tiles, peers, per, heads * HD)
    back = swap(jnp.swapaxes(att, 0, 1).reshape(rows, heads * HD)).reshape(rows, heads * HD)
    back = lax.all_gather(back, "tensor", axis=1, tiled=True)
    merged = jnp.dot(back, out_weight, preferred_element_type=jnp.float32)
    return (mine.astype(jnp.float32) + layer_scale.astype(jnp.float32) * merged).astype(jnp.bfloat16)


LINKS = 4


def fused(patches, rows, sides, w_hbm, ow_hbm, pos, out,
          own, mine, feats, w, ow, w_tail, qkv, att, ret, gain, scale,
          load, send, recv):
    n = own.shape[0]
    cols = patches.shape[0]
    per = patches.shape[1] // n
    full = cols // 128 * 128
    rest = cols - full
    steps = full // 128
    sums = steps * per + rest
    quarters = feats.shape[0]
    depth = w.shape[0]
    heads = w.shape[1] // (3 * HD)
    hw = heads * HD

    s = lax.axis_index("dp")
    t = lax.axis_index("tensor")
    z, core = lax.div(s, 2), lax.rem(s, 2)
    z_hi, z_lo = lax.div(z, 2), lax.rem(z, 2)
    y, x = lax.div(t, 2), lax.rem(t, 2)
    t_x = 2 * y + (1 - x)
    t_y = 2 * (1 - y) + x
    t_d = 2 * (1 - y) + (1 - x)

    def chip(j):
        return 2 * (z_hi if j < 2 else 1 - z_hi) + (z_lo if j % 2 == 0 else 1 - z_lo)

    def peer(k):
        return 2 * chip(k // 2) + (core if k % 2 == 0 else 1 - core)

    def remote(src, dst, kind, i, o, device):
        return pltpu.make_async_remote_copy(
            src_ref=src, dst_ref=dst, send_sem=send.at[kind, i], recv_sem=recv.at[kind, o],
            device_id=device, device_id_type=MESH)

    barrier = pltpu.get_barrier_semaphore()
    for k in range(1, n):
        pl.semaphore_signal(barrier, inc=1, device_id=(peer(k), t), device_id_type=MESH)
    for other in (t_x, t_y):
        pl.semaphore_signal(barrier, inc=1, device_id=(s, other), device_id_type=MESH)

    load_w = pltpu.make_async_copy(w_hbm, w, load.at[0])
    load_ow = pltpu.make_async_copy(ow_hbm, ow, load.at[1])
    load_w.start()
    load_ow.start()

    for which, wide in enumerate((gain, scale)):
        pick = lax.broadcasted_iota(jnp.int32, (16, 128), 0) == which
        pick = jnp.where(pick, 1.0, 0.0).astype(jnp.bfloat16)
        wide[...] = lax.dot_general(sides[...], pick, (((0,), (0,)), ((), ())), preferred_element_type=jnp.float32)

    def prepare(d):
        at = pl.ds(pl.multiple_of(d * per, per), per)
        idx = lax.rem(rows[pl.ds(d, 1), :], UNIT)
        hot = lax.broadcasted_iota(jnp.int32, (UNIT, per), 0) == idx
        hot = jnp.where(hot, 1.0, 0.0).astype(jnp.bfloat16)
        slot = jnp.dot(pos[...], hot, preferred_element_type=jnp.float32)
        row = (patches[:, at].astype(jnp.float32) + slot).astype(jnp.bfloat16)
        mine[:, at] = row
        row = row.astype(jnp.float32)
        square = jnp.sum(row * row, axis=0, keepdims=True)
        scaled = row * gain[...]
        for c in range(steps):
            own[d, c * per:(c + 1) * per, :] = scaled[c * 128:(c + 1) * 128].T.astype(jnp.bfloat16)
        own[d, steps * per:sums, :] = scaled[full:].astype(jnp.bfloat16)
        first = square.astype(jnp.bfloat16).astype(jnp.float32)
        second = (square - first).astype(jnp.bfloat16).astype(jnp.float32)
        third = square - first - second
        at_row = lax.broadcasted_iota(jnp.int32, (16, per), 0)
        last = jnp.where(at_row == 0, first, jnp.where(at_row == 1, second, jnp.where(at_row == 2, third, 0.0)))
        own[d, sums:, :] = last.astype(jnp.bfloat16)

    def scatter(buf, src, base, k):
        d = peer(k)
        remote(src.at[d], buf.at[t, s], base, d, s, (d, t)).start()

    def direct(buf, base, k):
        i = peer(k)
        if k > 0:
            remote(buf.at[t, i], buf.at[t, i], base, i, i, (s, t)).wait_recv()
        remote(buf.at[t, i], buf.at[t, i], base + 1, i, i, (s, t_x)).start()
        remote(buf.at[t, i], buf.at[t, i], base + 2, i, i, (s, t_y)).start()

    def relay(buf, base, k):
        i = peer(k)
        remote(buf.at[t, i], buf.at[t_x, i], base + 1, i, i, (s, t_x)).wait_recv()
        remote(buf.at[t, i], buf.at[t_y, i], base + 2, i, i, (s, t_y)).wait_recv()
        if k % 2 == 0:
            remote(buf.at[t_x, i], buf.at[t_x, i], base + 3, i, i, (s, t_y)).start()
        else:
            remote(buf.at[t_y, i], buf.at[t_y, i], base + 3, i, i, (s, t_x)).start()

    def settle(buf, base, k):
        i = peer(k)
        remote(buf.at[t_d, i], buf.at[t_d, i], base + 3, i, i, (s, t_x)).wait_recv()

    def project(j):
        settle(feats, 0, 2 * j)
        settle(feats, 0, 2 * j + 1)
        zj = chip(j)
        two = pl.ds(2 * zj, 2)
        at = pl.ds(pl.multiple_of(zj * 2 * per, 2 * per), 2 * per)
        def sides_of(low, high):
            return jnp.concatenate(
                [jnp.concatenate([feats[q, 2 * zj + c, low:high, :] for q in range(quarters)], axis=0) for c in range(2)], axis=1)

        tail = sides_of(steps * per, sums)
        square = lax.dot_general(sides_of(sums, sums + 16), jnp.ones((16 * quarters, 128), jnp.bfloat16),
                                 (((0,), (0,)), ((), ())), preferred_element_type=jnp.float32)
        norm = lax.rsqrt(square[:, :1] * (1.0 / depth) + EPS)

        def head(h, carry):
            span = pl.ds(pl.multiple_of(h * 3 * HD, 128), 3 * HD)
            acc = lax.dot_general(tail, w_tail[:, span], (((0,), (0,)), ((), ())), preferred_element_type=jnp.float32)
            for q in range(quarters):
                part = jnp.concatenate([feats[q, two, c * per:(c + 1) * per, :].reshape(2 * per, 128) for c in range(steps)], axis=1)
                acc += jnp.dot(part, w[q * cols:q * cols + full, span], preferred_element_type=jnp.float32)
            qkv[at, span] = (acc * norm).astype(jnp.bfloat16)
            return carry

        lax.fori_loop(0, heads, head, 0)

    def attend(j):
        zj = chip(j)
        at = pl.ds(pl.multiple_of(zj * 2 * per, 2 * per), 2 * per)

        def head(h, carry):
            q = qkv[at, pl.ds(pl.multiple_of(h * 3 * HD, 128), HD)]
            k = qkv[:, pl.ds(pl.multiple_of(h * 3 * HD + HD, 128), HD)]
            v = qkv[:, pl.ds(pl.multiple_of(h * 3 * HD + 2 * HD, 128), HD)]
            score = lax.dot_general(q, k, (((1,), (1,)), ((), ())), preferred_element_type=jnp.float32)
            peak = jnp.max(score, axis=-1, keepdims=True)
            e = jnp.exp2((score - peak) * (HD ** (-0.5) * 1.4426950408889634))
            total = jnp.sum(e, axis=-1, keepdims=True)
            o = jnp.dot(e.astype(jnp.bfloat16), v, preferred_element_type=jnp.float32) / total
            att[pl.ds(2 * zj, 2), :, pl.ds(pl.multiple_of(h * HD, 128), HD)] = o.astype(jnp.bfloat16).reshape(2, per, HD)
            return carry

        lax.fori_loop(0, heads, head, 0)

    def finish(j):
        settle(ret, LINKS, 2 * j)
        settle(ret, LINKS, 2 * j + 1)
        zj = chip(j)
        at = pl.ds(pl.multiple_of(zj * 2 * per, 2 * per), 2 * per)
        acc = jnp.zeros((cols, 2 * per), jnp.float32)
        for q in range(quarters):
            part = ret[q, pl.ds(2 * zj, 2)].reshape(2 * per, hw)
            acc += lax.dot_general(ow[:, q * hw:(q + 1) * hw], part, (((1,), (1,)), ((), ())), preferred_element_type=jnp.float32)
        level = jnp.concatenate([scale[...], scale[...]], axis=1)
        out[:, at] = (mine[:, at].astype(jnp.float32) + level * acc).astype(jnp.bfloat16)

    prepare(s)
    feats[t, s] = own[s]
    pl.semaphore_wait(barrier, n + 1)
    direct(feats, 0, 0)
    for k in range(1, n):
        prepare(peer(k))
        scatter(feats, own, 0, k)
    load_w.wait()
    for q in range(quarters):
        w_tail[q * rest:(q + 1) * rest, :] = w[q * cols + full:(q + 1) * cols, :]
    for k in range(1, n):
        direct(feats, 0, k)
        relay(feats, 0, k - 1)
        if k >= 3 and k % 2 == 1:
            project((k - 3) // 2)
    relay(feats, 0, n - 1)
    project(n // 2 - 1)

    pairs = n // 2
    load_ow.wait()
    for j in range(pairs + 2):
        if j < pairs:
            attend(j)
            for k in (2 * j, 2 * j + 1):
                if k == 0:
                    ret[t, s] = att[s]
                    direct(ret, LINKS, 0)
                else:
                    scatter(ret, att, LINKS, k)
            if j == 0:
                direct(ret, LINKS, 1)
        if 1 <= j <= pairs:
            for k in (2 * j - 2, 2 * j - 1):
                if k > 1:
                    direct(ret, LINKS, k)
            for k in (2 * j - 2, 2 * j - 1):
                relay(ret, LINKS, k)
        if j >= 2:
            finish(j - 2)

    for k in range(n):
        i = peer(k)
        for base, buf, src in ((0, feats, own), (LINKS, ret, att)):
            for kind in range(LINKS):
                if kind > 0 or k > 0:
                    whole = src.at[i] if kind == 0 else buf.at[t, i]
                    remote(whole, whole, base + kind, i, i, (s, t_x)).wait_send()


def one_kernel(patches, encoder_row, norm_gain, joint_weight, out_weight, layer_scale, pos_embed):
    n, quarters = lax.axis_size("dp"), lax.axis_size("tensor")
    rows, cols = patches.shape
    per = rows // n
    packed = cols // 128 * per + cols % 128 + 16
    hw = out_weight.shape[0] // quarters
    vmem = pl.BlockSpec(memory_space=pltpu.VMEM)
    hbm = pl.BlockSpec(memory_space=pl.ANY)
    bf16 = jnp.bfloat16
    sides = jnp.pad(jnp.stack([norm_gain, layer_scale]), ((0, 14), (0, 0)))
    result = pl.pallas_call(
        fused,
        out_shape=jax.ShapeDtypeStruct((cols, rows), bf16),
        in_specs=[vmem, vmem, vmem, hbm, hbm, vmem],
        out_specs=vmem,
        scratch_shapes=[
            pltpu.VMEM((n, packed, 128), bf16),
            pltpu.VMEM((cols, rows), bf16),
            pltpu.VMEM((quarters, n, packed, 128), bf16),
            pltpu.VMEM(joint_weight.shape, bf16),
            pltpu.VMEM((cols, quarters * hw), bf16),
            pltpu.VMEM((128, joint_weight.shape[1]), bf16),
            pltpu.VMEM((rows, joint_weight.shape[1]), bf16),
            pltpu.VMEM((n, per, hw), bf16),
            pltpu.VMEM((quarters, n, per, hw), bf16),
            pltpu.VMEM((cols, 128), jnp.float32),
            pltpu.VMEM((cols, 128), jnp.float32),
            pltpu.SemaphoreType.DMA((2,)),
            pltpu.SemaphoreType.DMA((2 * LINKS, n)),
            pltpu.SemaphoreType.DMA((2 * LINKS, n)),
        ],
        compiler_params=pltpu.CompilerParams(
            collective_id=0, has_side_effects=True, vmem_limit_bytes=60 * 1024 * 1024),
    )(patches.T, encoder_row.reshape(n, per), sides, joint_weight, out_weight.T, pos_embed.T)
    return result.T


def solution(mesh):
    fits = dict(mesh.shape) == dict(dp=8, tensor=4)
    body = one_kernel if fits else plain
    placed = (
        P("dp", "tensor"),
        P("dp"),
        P("tensor"),
        P(None, "tensor"),
        P(None, "tensor"),
        P("tensor"),
        P(None, "tensor"),
    )
    return jax.shard_map(
        body, mesh=mesh, in_specs=placed, out_specs=P("dp", "tensor"), check_vma=False
    )
```
